32 devices in a mesh: groups: 1, rows: 16 (over z, y, core), cols: 2 (over x), sub: 1.
Axes of the slice: x: 2, y: 2, z: 4, core: 2. Of those that a mesh axis runs over, the one named last changes fastest.
Arguments:
- activations: bfloat16 [4096, 5376], P(('groups', 'rows'), ('cols', 'sub')), may hold values from -40 to 40
- positions: int32 [4096], P('groups'), may hold values from 0 to 6143, as said below
- query_weight: bfloat16 [5376, 4096], P('rows', ('cols', 'sub')), may hold values from -0.078125 to 0.078125
- key_weight: bfloat16 [5376, 2048], P('rows', ('cols', 'sub')), may hold values from -0.078125 to 0.078125
- value_weight: bfloat16 [5376, 2048], P('rows', ('cols', 'sub')), may hold values from -0.078125 to 0.078125
- output_weight: bfloat16 [4096, 5376], P(('cols', 'sub'), 'rows'), may hold values from -0.09375 to 0.09375
- input_gain: float32 [5376], replicated, may hold values from 0.1 to 1.9
- query_gain: float32 [128], replicated, may hold values from 0.1 to 1.9
- key_gain: float32 [128], replicated, may hold values from 0.1 to 1.9
Outputs:
- attended: bfloat16 [4096, 5376], P(('groups', 'rows'), ('cols', 'sub'))
The draws below stay inside these ranges and needn't reach their ends.
Inputs may be any that keep to these rules, and one draw needn't show every extreme that they name: `positions`: position of each token in its document: it rises by one from token to token, or falls to 0 where a new document begins; the first document may begin at any position.
All inputs are finite; a program needn't handle non-finite values.
Results may differ from the reference program's by a relative error of at most 0.0065.
Values may be sent and summed in bfloat16 or wider, within the bound.
A program may use at most 128 MiB of HBM per device.

```python
import math
import jax
import jax.numpy as jnp
from jax import lax

D = 5376
HQ = 32
HK = 16
HD = 128
WINDOW = 1024
QUERY_SCALAR = 168
ROW_TOK = 256
SEQ = 4096
N_ROWS = 16
N_COLS = 2
N_SUB = 1


def draw_activations(key, part):
    data_key, row_key, column_key = jax.random.split(key, 3)
    values = jax.random.truncated_normal(data_key, -4.0, 4.0, (SEQ, D), jnp.float32)
    spread = 0.5
    row_scale = 10.0 ** jax.random.uniform(row_key, (SEQ, 1), jnp.float32, -spread, spread)
    column_scale = 10.0 ** jax.random.uniform(column_key, (1, D), jnp.float32, -0.5, 0.5)
    return (values * row_scale * column_scale).astype(jnp.bfloat16)


def draw_positions(key, part):
    mark_key, forced_key = jax.random.split(key, 2)
    indices = jnp.arange(SEQ, dtype=jnp.int32)
    marks = jax.random.randint(mark_key, (SEQ,), 0, 4 * WINDOW) == 0
    forced = jax.random.randint(forced_key, (), 1, SEQ)
    marks = (marks | (indices == forced)) & (indices > 0)
    latest = lax.cummax(jnp.where(marks, indices, 0), axis=0)
    first_mark = jnp.min(jnp.where(marks, indices, SEQ))
    offset = SEQ + 2 * WINDOW - first_mark
    return jnp.where(latest > 0, indices - latest, indices + offset).astype(jnp.int32)


def block_scale(stream_key, shape, shards, smallest, top_value):
    level, own = 1.0, jax.random.fold_in(stream_key, 6)
    for axis_at, parts in shards:
        steps = jnp.exp(jax.random.uniform(jax.random.fold_in(own, axis_at), (parts,), jnp.float32, smallest / len(shards), top_value / len(shards)))
        level = level * jnp.repeat(steps, shape[axis_at] // parts).reshape([-1 if axis == axis_at else 1 for axis in range(len(shape))])
    return level


def centred(stream_key, shape, deviation, reach, cuts=(), held_as=jnp.bfloat16):
    array = deviation * jax.random.normal(stream_key, shape, jnp.float32)
    if cuts:
        array = array * block_scale(stream_key, shape, cuts, -0.22, 0.18)
    return jnp.clip(array, -reach, reach).astype(held_as)


def setup_inputs(seed: int = 0, part: int = 0) -> dict:
    key_list = jax.random.split(jax.random.key(seed), 10)
    own_keys = jax.random.split(jax.random.fold_in(key_list[9], part), 10)
    return {
        "activations": draw_activations(jax.random.fold_in(jax.random.fold_in(key_list[9], part), 71), part),
        "positions": draw_positions(jax.random.fold_in(jax.random.fold_in(key_list[9], part), 71), part),
        "query_weight": centred(key_list[2], (D, HQ * HD), D ** -0.5, 0.078125, ((0, 16), (1, 2))),
        "key_weight": centred(key_list[3], (D, HK * HD), D ** -0.5, 0.078125, ((0, 16), (1, 2))),
        "value_weight": centred(key_list[4], (D, HK * HD), D ** -0.5, 0.078125, ((0, 16), (1, 2))),
        "output_weight": centred(key_list[5], (HQ * HD, D), (HQ * HD) ** -0.5, 0.09375, ((0, 2), (1, 16))),
        "input_gain": jnp.clip(1.0 + 0.18 * jax.random.normal(key_list[6], (D,), jnp.float32), 0.1, 1.9),
        "query_gain": jnp.clip(1.0 + 0.18 * jax.random.normal(key_list[7], (HD,), jnp.float32), 0.1, 1.9),
        "key_gain": jnp.clip(1.0 + 0.18 * jax.random.normal(key_list[8], (HD,), jnp.float32), 0.1, 1.9),
    }


def head_norm(tensor, gain_vector):
    return tensor * lax.rsqrt(lax.optimization_barrier(jnp.mean(tensor * tensor, axis=-1, keepdims=True)) + 1e-06) * gain_vector

def rotate(tensor, token_positions):
    half_width = tensor.shape[-1] // 2
    frequency = 10000.0 ** (-(jnp.arange(half_width, dtype=jnp.float32) * 2.0 / tensor.shape[-1]))
    angles = token_positions.astype(jnp.float32)[:, None] * frequency[None, :]
    cosine = jnp.cos(angles)[:, None, :]
    sine_part = jnp.sin(angles)[:, None, :]
    first_half = tensor[..., :half_width]
    second_half = tensor[..., half_width:]
    return jnp.concatenate([first_half * cosine - second_half * sine_part, second_half * cosine + first_half * sine_part], axis=-1)

def attend(queries, key_rows, value_rows, query_index, key_index, query_pos, key_pos):
    row_count = queries.shape[0]
    key_count = key_rows.shape[0]
    kv_heads = key_rows.shape[1] // HD
    group_size = queries.shape[1] // key_rows.shape[1]
    query_four = queries.astype(jnp.float32).reshape(row_count, kv_heads, group_size, HD)
    key_three = key_rows.astype(jnp.float32).reshape(key_count, kv_heads, HD)
    value_three = value_rows.astype(jnp.float32).reshape(key_count, kv_heads, HD)
    score_scale = 1.0 / math.sqrt(QUERY_SCALAR)
    scores = jnp.einsum('qgrd,kgd->grqk', query_four, key_three) * score_scale
    distance = query_index[:, None] - key_index[None, :]
    visible = (key_index[None, :] >= 0) & (distance >= 0) & (distance < WINDOW) & (query_pos[:, None] - key_pos[None, :] == distance)
    weights = jnp.where(visible[None, None], jnp.exp(scores), 0.0)
    totals = lax.optimization_barrier(jnp.sum(weights, axis=-1))
    rounded = lax.optimization_barrier(weights.astype(jnp.bfloat16))
    mixed_heads = jnp.einsum('grqk,kgd->qgrd', rounded.astype(jnp.float32), value_three)
    mixed_heads = mixed_heads / jnp.transpose(totals, (2, 0, 1))[..., None]
    return mixed_heads.astype(jnp.bfloat16).reshape(row_count, kv_heads * group_size * HD)

def reference(activations, positions, query_weight, key_weight, value_weight, output_weight, input_gain, query_gain, key_gain):
    widened = activations.astype(jnp.float32)
    inverse = lax.rsqrt(lax.optimization_barrier(jnp.mean(widened * widened, axis=-1, keepdims=True)) + 1e-06)
    normed = (widened * inverse * input_gain).astype(jnp.bfloat16)
    query_raw = jnp.dot(normed, query_weight, preferred_element_type=jnp.float32)
    key_raw = jnp.dot(normed, key_weight, preferred_element_type=jnp.float32)
    value_rows = jnp.dot(normed, value_weight, preferred_element_type=jnp.float32).astype(jnp.bfloat16)
    queries = rotate(head_norm(query_raw.reshape(SEQ, HQ, HD), query_gain), positions).astype(jnp.bfloat16).reshape(SEQ, HQ * HD)
    key_rows = rotate(head_norm(key_raw.reshape(SEQ, HK, HD), key_gain), positions).astype(jnp.bfloat16).reshape(SEQ, HK * HD)
    reach_rows = -(-WINDOW // ROW_TOK)
    margin = reach_rows * ROW_TOK
    key_padded = jnp.concatenate([jnp.zeros((margin, HK * HD), jnp.bfloat16), key_rows], axis=0)
    value_padded = jnp.concatenate([jnp.zeros((margin, HK * HD), jnp.bfloat16), value_rows], axis=0)
    position_padded = jnp.concatenate([jnp.zeros((margin,), jnp.int32), positions.astype(jnp.int32)], axis=0)

    def one_block(block_index):
        first_row = (block_index * ROW_TOK).astype(jnp.int32)
        query_block = lax.dynamic_slice_in_dim(queries, first_row, ROW_TOK, 0)
        key_block = lax.dynamic_slice_in_dim(key_padded, first_row, ROW_TOK + margin, 0)
        value_block = lax.dynamic_slice_in_dim(value_padded, first_row, ROW_TOK + margin, 0)
        query_pos = lax.dynamic_slice_in_dim(positions.astype(jnp.int32), first_row, ROW_TOK, 0)
        key_pos = lax.dynamic_slice_in_dim(position_padded, first_row, ROW_TOK + margin, 0)
        query_index = first_row + jnp.arange(ROW_TOK, dtype=jnp.int32)
        key_index = first_row - margin + jnp.arange(ROW_TOK + margin, dtype=jnp.int32)
        return attend(query_block, key_block, value_block, query_index, key_index, query_pos, key_pos)
    context = lax.map(one_block, jnp.arange(N_ROWS, dtype=jnp.int32)).reshape(SEQ, HQ * HD)
    groups_count = N_COLS * N_SUB
    group_width = HQ * HD // groups_count
    summed = widened
    for group in range(groups_count):
        lower = group * group_width
        upper = lower + group_width
        partial_sum = jnp.dot(context[:, lower:upper], output_weight[lower:upper], preferred_element_type=jnp.float32).astype(jnp.bfloat16)
        partial_sum = lax.optimization_barrier(partial_sum)
        summed = summed + partial_sum.astype(jnp.float32)
    return summed.astype(jnp.bfloat16)
```

```python
import functools
import math

import jax
import jax.numpy as jnp
from jax import lax
from jax.experimental import pallas as pl
from jax.experimental.pallas import tpu as pltpu
from jax.sharding import Mesh
from jax.sharding import PartitionSpec as P

HD = 128
WINDOW = 1024
QUERY_SCALAR = 168


def passed_along(value, axis, by):
    peers = lax.axis_size(axis)
    pairs = [(i, i + by) for i in range(peers) if 0 <= i + by < peers]
    return lax.ppermute(value, axis, pairs)


def head_norm(tensor, gain_vector):
    return (
        tensor * lax.rsqrt(jnp.mean(tensor * tensor, axis=-1, keepdims=True) + 1e-06) * gain_vector
    )


def rotate(tensor, token_positions):
    half_width = tensor.shape[-1] // 2
    frequency = 10000.0 ** (-(jnp.arange(half_width, dtype=jnp.float32) * 2.0 / tensor.shape[-1]))
    angles = token_positions.astype(jnp.float32)[:, None] * frequency[None, :]
    cosine = jnp.cos(angles)[:, None, :]
    sine_part = jnp.sin(angles)[:, None, :]
    first_half = tensor[..., :half_width]
    second_half = tensor[..., half_width:]
    return jnp.concatenate(
        [
            first_half * cosine - second_half * sine_part,
            second_half * cosine + first_half * sine_part,
        ],
        axis=-1,
    )


def attend(queries, key_rows, value_rows, query_index, key_index, query_pos, key_pos):
    row_count = queries.shape[0]
    key_count = key_rows.shape[0]
    kv_heads = key_rows.shape[1] // HD
    group_size = queries.shape[1] // key_rows.shape[1]
    query_four = queries.reshape(row_count, kv_heads, group_size, HD)
    key_three = key_rows.reshape(key_count, kv_heads, HD)
    value_three = value_rows.reshape(key_count, kv_heads, HD)
    score_scale = 1.0 / math.sqrt(QUERY_SCALAR)
    scores = (
        jnp.einsum("qgrd,kgd->grqk", query_four, key_three, preferred_element_type=jnp.float32)
        * score_scale
    )
    distance = query_index[:, None] - key_index[None, :]
    visible = (
        (key_index[None, :] >= 0)
        & (distance >= 0)
        & (distance < WINDOW)
        & (query_pos[:, None] - key_pos[None, :] == distance)
    )
    weights = jnp.where(visible[None, None], jnp.exp(scores), 0.0)
    totals = jnp.sum(weights, axis=-1)
    rounded = weights.astype(jnp.bfloat16)
    mixed_heads = jnp.einsum(
        "grqk,kgd->qgrd", rounded, value_three, preferred_element_type=jnp.float32
    )
    mixed_heads = mixed_heads / jnp.transpose(totals, (2, 0, 1))[..., None]
    return mixed_heads.astype(jnp.bfloat16).reshape(row_count, kv_heads * group_size * HD)


def reach_back(key_rows, value_rows, reach_rows):
    pieces = []
    carried = (key_rows, value_rows)
    for distance in range(reach_rows):
        carried = passed_along((carried[0], carried[1]), "rows", 1)
        pieces.append(carried)
    ordered = pieces[::-1] + [(key_rows, value_rows)]
    all_keys = jnp.concatenate([member[0] for member in ordered], axis=0)
    all_values = jnp.concatenate([member[1] for member in ordered], axis=0)
    return (all_keys, all_values)


def body(
    activations,
    positions,
    query_weight,
    key_weight,
    value_weight,
    output_weight,
    input_gain,
    query_gain,
    key_gain,
):
    rows_here = activations.shape[0]
    row_panel = lax.all_gather(activations, ("cols", "sub"), axis=1, tiled=True)
    panel_wide = row_panel.astype(jnp.float32)
    inverse = lax.rsqrt(jnp.mean(panel_wide * panel_wide, axis=-1, keepdims=True) + 1e-06)
    normed = (panel_wide * inverse * input_gain).astype(jnp.bfloat16)
    row_index = lax.axis_index("rows")
    own_positions = lax.dynamic_slice_in_dim(positions, row_index * rows_here, rows_here, 0)
    reach_rows = min(-(-WINDOW // rows_here), lax.axis_size("rows") - 1)

    def add_rows(weight_piece):
        return jnp.dot(normed, weight_piece, preferred_element_type=jnp.float32)

    weight_piece = (
        lax.all_gather(query_weight, "rows", axis=0, tiled=True),
        lax.all_gather(key_weight, "rows", axis=0, tiled=True),
        lax.all_gather(value_weight, "rows", axis=0, tiled=True),
    )
    query_raw = add_rows(weight_piece[0])
    key_raw = add_rows(weight_piece[1])
    value_raw = add_rows(weight_piece[2])
    key_rows = rotate(head_norm(key_raw.reshape(rows_here, -1, HD), key_gain), own_positions)
    key_rows, value_rows = (
        key_rows.astype(jnp.bfloat16).reshape(rows_here, -1),
        value_raw.astype(jnp.bfloat16),
    )
    all_keys, all_values = reach_back(key_rows, value_rows, reach_rows)
    queries = rotate(head_norm(query_raw.reshape(rows_here, -1, HD), query_gain), own_positions)
    queries = queries.astype(jnp.bfloat16).reshape(rows_here, -1)
    key_count = all_keys.shape[0]
    query_index = row_index * rows_here + jnp.arange(rows_here, dtype=jnp.int32)
    key_index = (row_index - reach_rows) * rows_here + jnp.arange(key_count, dtype=jnp.int32)
    padded = jnp.concatenate([jnp.zeros((reach_rows * rows_here,), jnp.int32), positions], axis=0)
    key_positions = lax.dynamic_slice_in_dim(padded, row_index * rows_here, key_count, 0)
    context = attend(
        queries, all_keys, all_values, query_index, key_index, own_positions, key_positions
    )
    partial_terms = jnp.dot(
        context,
        lax.all_gather(output_weight, "rows", axis=1, tiled=True),
        preferred_element_type=jnp.float32,
    )
    summed = lax.psum_scatter(
        partial_terms.astype(jnp.bfloat16), ("cols", "sub"), scatter_dimension=1, tiled=True
    ).astype(jnp.float32)
    return (activations.astype(jnp.float32) + summed).astype(jnp.bfloat16)


def row_solution(mesh):
    placed = (
        P(("groups", "rows"), ("cols", "sub")),
        P("groups"),
        P("rows", ("cols", "sub")),
        P("rows", ("cols", "sub")),
        P("rows", ("cols", "sub")),
        P(("cols", "sub"), "rows"),
        P(),
        P(),
        P(),
    )
    return jax.shard_map(
        body,
        mesh=mesh,
        in_specs=placed,
        out_specs=P(("groups", "rows"), ("cols", "sub")),
        check_vma=False,
    )

def flipped(value, axis):
    return lax.ppermute(value, axis, [(0, 1), (1, 0)])


def pick(array, index, axis):
    return lax.dynamic_index_in_dim(array, index, axis, keepdims=False)


def reduce_in_plane(terms, width_here):
    rows = terms.shape[0] // 4
    mid, low, col = lax.axis_index("mid"), lax.axis_index("low"), lax.axis_index("cols")
    four = terms.reshape(2, 2, rows, -1)
    got = flipped(pick(four, 1 - low, 1), "low")
    chip = (pick(four, low, 1).astype(jnp.float32) + got.astype(jnp.float32)).astype(jnp.bfloat16)

    def columns(array, index):
        return lax.dynamic_slice_in_dim(array, index * width_here, width_here, array.ndim - 1)

    def added(a, b):
        return a.astype(jnp.float32) + b.astype(jnp.float32)

    first, second = chip[:, : rows // 2], chip[:, rows // 2 :]
    got_a = flipped(columns(first, 1 - col), "cols")
    got_b = flipped(pick(second, 1 - mid, 0), "mid")
    part_a = added(columns(first, col), got_a).astype(jnp.bfloat16)
    part_b = added(pick(second, mid, 0), got_b).astype(jnp.bfloat16)
    got_a = flipped(pick(part_a, 1 - mid, 0), "mid")
    got_b = flipped(columns(part_b, 1 - col), "cols")
    return jnp.concatenate(
        [added(pick(part_a, mid, 0), got_a), added(columns(part_b, col), got_b)], axis=0
    )


def gather_kernel(planes, count, *refs):
    weights, tokens = refs[:count], refs[count]
    fulls, panel = refs[count + 1 : 2 * count + 1], refs[2 * count + 1]
    (own_sem, deal_send, deal_recv, up_send, up_recv, down_send, down_recv) = refs[
        2 * count + 2 : 2 * count + 9
    ]
    act_own, act_send, act_recv = refs[2 * count + 9 :]
    own = lax.axis_index("outer")
    mid, low, col = lax.axis_index("mid"), lax.axis_index("low"), lax.axis_index("cols")
    mids, lows, sides = (mid, 1 - mid), (low, 1 - low), (col, 1 - col)
    depth = weights[0].shape[0]
    rows = tokens.shape[0]
    has_up, has_down = own < planes - 1, own > 0

    def plane_peer(k):
        return {"mid": mids[k // 2], "low": lows[k % 2]}

    def place(k):
        return mids[k // 2] * 2 + lows[k % 2]

    barrier = pltpu.get_barrier_semaphore()
    for k in range(8):
        if k:
            pl.semaphore_signal(
                barrier,
                inc=1,
                device_id=dict(plane_peer(k % 4), cols=sides[k // 4]),
                device_id_type=pl.DeviceIdType.MESH,
            )

    @pl.when(has_up)
    def _():
        pl.semaphore_signal(
            barrier, inc=1, device_id={"outer": own + 1}, device_id_type=pl.DeviceIdType.MESH
        )

    @pl.when(has_down)
    def _():
        pl.semaphore_signal(
            barrier, inc=1, device_id={"outer": own - 1}, device_id_type=pl.DeviceIdType.MESH
        )

    pl.semaphore_wait(barrier, 7 + jnp.where(has_up, 1, 0) + jnp.where(has_down, 1, 0))

    def block(t, plane, k):
        at = pl.multiple_of((plane * 4 + place(k)) * depth, 16)
        return fulls[t].at[pl.ds(at, depth), :]

    def own_block(t):
        at = pl.multiple_of((own * 4 + mid * 2 + low) * depth, 16)
        return fulls[t].at[pl.ds(at, depth), :]

    def part(t, k):
        wide = fulls[t].shape[1]
        return weights[t].at[:, pl.ds(pl.multiple_of(place(k) * wide, 128), wide)]

    def local(t):
        return pltpu.make_async_copy(part(t, 0), own_block(t), own_sem.at[t])

    def deal(t, k):
        return pltpu.make_async_remote_copy(
            src_ref=part(t, k),
            dst_ref=own_block(t),
            send_sem=deal_send.at[t, k],
            recv_sem=deal_recv.at[t, k],
            device_id=plane_peer(k),
            device_id_type=pl.DeviceIdType.MESH,
        )

    def passed(t, d, k, step, sends, recvs):
        where = block(t, jnp.clip(own - step * d, 0, planes - 1), k)
        return pltpu.make_async_remote_copy(
            src_ref=where,
            dst_ref=where,
            send_sem=sends.at[t, d, k],
            recv_sem=recvs.at[t, d, k],
            device_id={"outer": jnp.clip(own + step, 0, planes - 1)},
            device_id_type=pl.DeviceIdType.MESH,
        )

    def up(t, d, k):
        return passed(t, d, k, 1, up_send, up_recv)

    def down(t, d, k):
        return passed(t, d, k, -1, down_send, down_recv)

    def share(k):
        at = pl.multiple_of((mid * 2 + low) * rows, 16)
        where = panel.at[col, pl.ds(at, rows), :]
        if k == 0:
            return pltpu.make_async_copy(tokens, where, act_own.at[0])
        return pltpu.make_async_remote_copy(
            src_ref=tokens,
            dst_ref=where,
            send_sem=act_send.at[k],
            recv_sem=act_recv.at[k],
            device_id=dict(plane_peer(k % 4), cols=sides[k // 4]),
            device_id_type=pl.DeviceIdType.MESH,
        )

    for t in range(count):
        local(t).start()
    for k in (2, 3, 1):
        for t in range(count):
            deal(t, k).start()
    for d in range(planes):
        for k in (0, 1, 2, 3):
            for t in range(count):
                if d == 0:
                    if k == 0:
                        local(t).wait()
                    else:
                        deal(t, k).wait_recv()
                if d > 0:

                    @pl.when(own - d >= 0)
                    def _():
                        up(t, d - 1, k).wait_recv()

                    @pl.when(own + d < planes)
                    def _():
                        down(t, d - 1, k).wait_recv()

                if d < planes - 1:

                    @pl.when((own - d >= 0) & has_up)
                    def _():
                        up(t, d, k).start()

                    @pl.when((own + d < planes) & has_down)
                    def _():
                        down(t, d, k).start()

        if d == 0:
            for k in (4, 5, 6, 7, 2, 3, 1, 0):
                share(k).start()
    for d in range(planes - 1):
        for k in range(4):
            for t in range(count):

                @pl.when((own - d >= 0) & has_up)
                def _():
                    up(t, d, k).wait_send()

                @pl.when((own + d < planes) & has_down)
                def _():
                    down(t, d, k).wait_send()

    for k in (1, 2, 3):
        for t in range(count):
            deal(t, k).wait_send()
    share(0).wait()
    for k in range(1, 8):
        share(k).wait()


def gather_all(weights, tokens):
    planes = lax.axis_size("outer")
    count = len(weights)
    depth = weights[0].shape[0]
    anywhere = pl.BlockSpec(memory_space=pl.ANY)
    line = pltpu.SemaphoreType.DMA((count, planes - 1, 4))
    shapes = [
        jax.ShapeDtypeStruct((planes * 4 * depth, weight.shape[1] // 4), weight.dtype)
        for weight in weights
    ]
    shapes.append(jax.ShapeDtypeStruct((2, 4 * tokens.shape[0], tokens.shape[1]), tokens.dtype))
    return pl.pallas_call(
        functools.partial(gather_kernel, planes, count),
        out_shape=shapes,
        in_specs=[anywhere] * (count + 1),
        out_specs=[anywhere] * (count + 1),
        scratch_shapes=[
            pltpu.SemaphoreType.DMA((count,)),
            pltpu.SemaphoreType.DMA((count, 4)),
            pltpu.SemaphoreType.DMA((count, 4)),
            line,
            line,
            line,
            line,
            pltpu.SemaphoreType.DMA((1,)),
            pltpu.SemaphoreType.DMA((8,)),
            pltpu.SemaphoreType.DMA((8,)),
        ],
        compiler_params=pltpu.CompilerParams(collective_id=0, has_side_effects=True),
        cost_estimate=pl.CostEstimate(
            flops=200_000_000_000, bytes_accessed=600_000_000, transcendentals=0
        ),
        name="gather_weights",
    )(*weights, tokens)


def plane_body(
    activations,
    positions,
    query_weight,
    key_weight,
    value_weight,
    output_weight,
    input_gain,
    query_gain,
    key_gain,
):
    rows_here, width_here = activations.shape
    inner = 4
    plane_tokens = inner * rows_here
    key_full, value_full, query_full, output_full, panel = gather_all(
        [key_weight, value_weight, query_weight, output_weight.T], activations
    )
    left, right = panel[0].astype(jnp.float32), panel[1].astype(jnp.float32)
    squares = jnp.sum(left * left, axis=-1) + jnp.sum(right * right, axis=-1)
    inverse = lax.rsqrt(squares[:, None] / (2 * width_here) + 1e-06)
    normed_left = (left * inverse * input_gain[:width_here]).astype(jnp.bfloat16)
    normed_right = (right * inverse * input_gain[width_here:]).astype(jnp.bfloat16)
    outer_index = lax.axis_index("outer")
    first = outer_index * plane_tokens
    own_positions = lax.dynamic_slice_in_dim(positions, first, plane_tokens, 0)

    def project(weight):
        return jnp.dot(
            normed_left, weight[:width_here], preferred_element_type=jnp.float32
        ) + jnp.dot(normed_right, weight[width_here:], preferred_element_type=jnp.float32)

    key_raw = project(key_full)
    keys = rotate(head_norm(key_raw.reshape(plane_tokens, -1, HD), key_gain), own_positions)
    keys = keys.astype(jnp.bfloat16).reshape(plane_tokens, -1)
    keys_before = passed_along(keys[plane_tokens - WINDOW :], "outer", 1)
    values = project(value_full).astype(jnp.bfloat16)
    values_before = passed_along(values[plane_tokens - WINDOW :], "outer", 1)
    all_keys = jnp.concatenate([keys_before, keys], axis=0)
    all_values = jnp.concatenate([values_before, values], axis=0)
    queries = rotate(
        head_norm(project(query_full).reshape(plane_tokens, -1, HD), query_gain), own_positions
    )
    queries = queries.astype(jnp.bfloat16).reshape(plane_tokens, -1)
    padded = jnp.concatenate([jnp.zeros((WINDOW,), jnp.int32), positions], axis=0)
    key_positions = lax.dynamic_slice_in_dim(padded, first, plane_tokens + WINDOW, 0)
    count = rows_here + WINDOW
    contexts = []
    for block in range(inner):
        at = block * rows_here
        contexts.append(
            attend(
                queries[at : at + rows_here],
                all_keys[at : at + count],
                all_values[at : at + count],
                first + at + jnp.arange(rows_here, dtype=jnp.int32),
                first + at - WINDOW + jnp.arange(count, dtype=jnp.int32),
                own_positions[at : at + rows_here],
                key_positions[at : at + count],
            )
        )
    context = jnp.concatenate(contexts, axis=0)
    terms = lax.dot_general(
        context, output_full, (((1,), (1,)), ((), ())), preferred_element_type=jnp.float32
    ).astype(jnp.bfloat16)
    summed = reduce_in_plane(terms, width_here)
    return (activations.astype(jnp.float32) + summed).astype(jnp.bfloat16)


def plane_solution(mesh):
    sizes = mesh.shape
    split = Mesh(
        mesh.devices.reshape(
            sizes["groups"], sizes["rows"] // 4, 2, 2, sizes["cols"], sizes["sub"]
        ),
        ("groups", "outer", "mid", "low", "cols", "sub"),
    )
    rows, cols = ("outer", "mid", "low"), ("cols", "sub")
    placed = (
        P(("groups",) + rows, cols),
        P("groups"),
        P(rows, cols),
        P(rows, cols),
        P(rows, cols),
        P(cols, rows),
        P(),
        P(),
        P(),
    )
    return jax.shard_map(
        plane_body,
        mesh=split,
        in_specs=placed,
        out_specs=P(("groups",) + rows, cols),
        check_vma=False,
    )


def solution(mesh):
    sizes = mesh.shape
    parts = sizes["cols"] * sizes["sub"]

    def run(*args):
        tokens = args[0].shape[0] // (sizes["groups"] * sizes["rows"])
        kv_heads = args[3].shape[1] // (HD * parts)
        fits = sizes["rows"] % (4 * parts) == 0 and kv_heads % 4 == 0
        fits = fits and sizes["cols"] == 2 and sizes["sub"] == 1 and tokens * 4 >= WINDOW
        plan = plane_solution(mesh) if fits else row_solution(mesh)
        return plan(*args)

    return run
```

```python
import functools
import math

import jax
import jax.numpy as jnp
from jax import lax
from jax.experimental import pallas as pl
from jax.experimental.pallas import tpu as pltpu
from jax.sharding import Mesh
from jax.sharding import PartitionSpec as P

HD = 128
WINDOW = 1024
QUERY_SCALAR = 168


def passed_along(value, axis, by):
    peers = lax.axis_size(axis)
    pairs = [(i, i + by) for i in range(peers) if 0 <= i + by < peers]
    return lax.ppermute(value, axis, pairs)


def head_norm(tensor, gain_vector):
    return (
        tensor * lax.rsqrt(jnp.mean(tensor * tensor, axis=-1, keepdims=True) + 1e-06) * gain_vector
    )


def rotate(tensor, token_positions):
    half_width = tensor.shape[-1] // 2
    frequency = 10000.0 ** (-(jnp.arange(half_width, dtype=jnp.float32) * 2.0 / tensor.shape[-1]))
    angles = token_positions.astype(jnp.float32)[:, None] * frequency[None, :]
    cosine = jnp.cos(angles)[:, None, :]
    sine_part = jnp.sin(angles)[:, None, :]
    first_half = tensor[..., :half_width]
    second_half = tensor[..., half_width:]
    return jnp.concatenate(
        [
            first_half * cosine - second_half * sine_part,
            second_half * cosine + first_half * sine_part,
        ],
        axis=-1,
    )


def attend(queries, key_rows, value_rows, query_index, key_index, query_pos, key_pos):
    row_count = queries.shape[0]
    key_count = key_rows.shape[0]
    kv_heads = key_rows.shape[1] // HD
    group_size = queries.shape[1] // key_rows.shape[1]
    query_four = queries.reshape(row_count, kv_heads, group_size, HD)
    key_three = key_rows.reshape(key_count, kv_heads, HD)
    value_three = value_rows.reshape(key_count, kv_heads, HD)
    score_scale = 1.0 / math.sqrt(QUERY_SCALAR)
    scores = (
        jnp.einsum("qgrd,kgd->grqk", query_four, key_three, preferred_element_type=jnp.float32)
        * score_scale
    )
    distance = query_index[:, None] - key_index[None, :]
    visible = (
        (key_index[None, :] >= 0)
        & (distance >= 0)
        & (distance < WINDOW)
        & (query_pos[:, None] - key_pos[None, :] == distance)
    )
    weights = jnp.where(visible[None, None], jnp.exp(scores), 0.0)
    totals = jnp.sum(weights, axis=-1)
    rounded = weights.astype(jnp.bfloat16)
    mixed_heads = jnp.einsum(
        "grqk,kgd->qgrd", rounded, value_three, preferred_element_type=jnp.float32
    )
    mixed_heads = mixed_heads / jnp.transpose(totals, (2, 0, 1))[..., None]
    return mixed_heads.astype(jnp.bfloat16).reshape(row_count, kv_heads * group_size * HD)


def reach_back(key_rows, value_rows, reach_rows):
    pieces = []
    carried = (key_rows, value_rows)
    for distance in range(reach_rows):
        carried = passed_along((carried[0], carried[1]), "rows", 1)
        pieces.append(carried)
    ordered = pieces[::-1] + [(key_rows, value_rows)]
    all_keys = jnp.concatenate([member[0] for member in ordered], axis=0)
    all_values = jnp.concatenate([member[1] for member in ordered], axis=0)
    return (all_keys, all_values)


def body(
    activations,
    positions,
    query_weight,
    key_weight,
    value_weight,
    output_weight,
    input_gain,
    query_gain,
    key_gain,
):
    rows_here = activations.shape[0]
    row_panel = lax.all_gather(activations, ("cols", "sub"), axis=1, tiled=True)
    panel_wide = row_panel.astype(jnp.float32)
    inverse = lax.rsqrt(jnp.mean(panel_wide * panel_wide, axis=-1, keepdims=True) + 1e-06)
    normed = (panel_wide * inverse * input_gain).astype(jnp.bfloat16)
    row_index = lax.axis_index("rows")
    own_positions = lax.dynamic_slice_in_dim(positions, row_index * rows_here, rows_here, 0)
    reach_rows = min(-(-WINDOW // rows_here), lax.axis_size("rows") - 1)

    def add_rows(weight_piece):
        return jnp.dot(normed, weight_piece, preferred_element_type=jnp.float32)

    weight_piece = (
        lax.all_gather(query_weight, "rows", axis=0, tiled=True),
        lax.all_gather(key_weight, "rows", axis=0, tiled=True),
        lax.all_gather(value_weight, "rows", axis=0, tiled=True),
    )
    query_raw = add_rows(weight_piece[0])
    key_raw = add_rows(weight_piece[1])
    value_raw = add_rows(weight_piece[2])
    key_rows = rotate(head_norm(key_raw.reshape(rows_here, -1, HD), key_gain), own_positions)
    key_rows, value_rows = (
        key_rows.astype(jnp.bfloat16).reshape(rows_here, -1),
        value_raw.astype(jnp.bfloat16),
    )
    all_keys, all_values = reach_back(key_rows, value_rows, reach_rows)
    queries = rotate(head_norm(query_raw.reshape(rows_here, -1, HD), query_gain), own_positions)
    queries = queries.astype(jnp.bfloat16).reshape(rows_here, -1)
    key_count = all_keys.shape[0]
    query_index = row_index * rows_here + jnp.arange(rows_here, dtype=jnp.int32)
    key_index = (row_index - reach_rows) * rows_here + jnp.arange(key_count, dtype=jnp.int32)
    padded = jnp.concatenate([jnp.zeros((reach_rows * rows_here,), jnp.int32), positions], axis=0)
    key_positions = lax.dynamic_slice_in_dim(padded, row_index * rows_here, key_count, 0)
    context = attend(
        queries, all_keys, all_values, query_index, key_index, own_positions, key_positions
    )
    partial_terms = jnp.dot(
        context,
        lax.all_gather(output_weight, "rows", axis=1, tiled=True),
        preferred_element_type=jnp.float32,
    )
    summed = lax.psum_scatter(
        partial_terms.astype(jnp.bfloat16), ("cols", "sub"), scatter_dimension=1, tiled=True
    ).astype(jnp.float32)
    return (activations.astype(jnp.float32) + summed).astype(jnp.bfloat16)


def row_solution(mesh):
    placed = (
        P(("groups", "rows"), ("cols", "sub")),
        P("groups"),
        P("rows", ("cols", "sub")),
        P("rows", ("cols", "sub")),
        P("rows", ("cols", "sub")),
        P(("cols", "sub"), "rows"),
        P(),
        P(),
        P(),
    )
    return jax.shard_map(
        body,
        mesh=mesh,
        in_specs=placed,
        out_specs=P(("groups", "rows"), ("cols", "sub")),
        check_vma=False,
    )

def flipped(value, axis):
    return lax.ppermute(value, axis, [(0, 1), (1, 0)])


def pick(array, index, axis):
    return lax.dynamic_index_in_dim(array, index, axis, keepdims=False)


def along_line(block):
    planes = lax.axis_size("outer")
    own = lax.axis_index("outer")
    up, down = [block], [block]
    for _ in range(planes - 1):
        up.append(lax.ppermute(up[-1], "outer", [(i, i + 1) for i in range(planes - 1)]))
        down.append(lax.ppermute(down[-1], "outer", [(i + 1, i) for i in range(planes - 1)]))
    return [jnp.where(own >= d, up[d], down[planes - d]) for d in range(1, planes)]


def plane_of(d):
    planes = lax.axis_size("outer")
    return lax.rem(lax.axis_index("outer") - d + planes, planes)


def reduce_in_plane(first, second, width_here):
    mid, low, col = lax.axis_index("mid"), lax.axis_index("low"), lax.axis_index("cols")

    def columns(array, index):
        return lax.dynamic_slice_in_dim(array, index * width_here, width_here, array.ndim - 1)

    def added(a, b):
        return a.astype(jnp.float32) + b.astype(jnp.float32)

    def chip_sum(terms):
        got = flipped(pick(terms, 1 - low, 1), "low")
        return added(pick(terms, low, 1), got).astype(jnp.bfloat16)

    first = chip_sum(first)
    got_a = flipped(columns(first, 1 - col), "cols")
    second = chip_sum(second)
    got_b = flipped(pick(second, 1 - mid, 0), "mid")
    part_a = added(columns(first, col), got_a).astype(jnp.bfloat16)
    part_b = added(pick(second, mid, 0), got_b).astype(jnp.bfloat16)
    got_a = flipped(pick(part_a, 1 - mid, 0), "mid")
    got_b = flipped(columns(part_b, 1 - col), "cols")
    return jnp.concatenate(
        [added(pick(part_a, mid, 0), got_a), added(columns(part_b, col), got_b)], axis=0
    )


def gather_kernel(planes, count, relayed, *refs):
    weights, tokens = refs[:count], refs[count]
    fulls, panel = refs[count + 1 : 2 * count + 1], refs[2 * count + 1]
    (own_sem, deal_send, deal_recv, up_send, up_recv, down_send, down_recv) = refs[
        2 * count + 2 : 2 * count + 9
    ]
    act_own, act_send, act_recv = refs[2 * count + 9 :]
    own = lax.axis_index("outer")
    mid, low, col = lax.axis_index("mid"), lax.axis_index("low"), lax.axis_index("cols")
    mids, lows, sides = (mid, 1 - mid), (low, 1 - low), (col, 1 - col)
    depth = weights[0].shape[0]
    rows = tokens.shape[0]
    has_up, has_down = own < planes - 1, own > 0

    def plane_peer(k):
        return {"mid": mids[k // 2], "low": lows[k % 2]}

    def place(k):
        return mids[k // 2] * 2 + lows[k % 2]

    barrier = pltpu.get_barrier_semaphore()
    for k in range(8):
        if k:
            pl.semaphore_signal(
                barrier,
                inc=1,
                device_id=dict(plane_peer(k % 4), cols=sides[k // 4]),
                device_id_type=pl.DeviceIdType.MESH,
            )

    @pl.when(has_up)
    def _():
        pl.semaphore_signal(
            barrier, inc=1, device_id={"outer": own + 1}, device_id_type=pl.DeviceIdType.MESH
        )

    @pl.when(has_down)
    def _():
        pl.semaphore_signal(
            barrier, inc=1, device_id={"outer": own - 1}, device_id_type=pl.DeviceIdType.MESH
        )

    pl.semaphore_wait(barrier, 7 + jnp.where(has_up, 1, 0) + jnp.where(has_down, 1, 0))

    def block(t, plane, k):
        at = pl.multiple_of((plane * 4 + place(k)) * depth, 16)
        return fulls[t].at[pl.ds(at, depth), :]

    def own_block(t):
        at = pl.multiple_of((own * 4 + mid * 2 + low) * depth, 16)
        return fulls[t].at[pl.ds(at, depth), :]

    def part(t, k):
        wide = fulls[t].shape[1]
        return weights[t].at[:, pl.ds(pl.multiple_of(place(k) * wide, 128), wide)]

    def local(t):
        return pltpu.make_async_copy(part(t, 0), own_block(t), own_sem.at[t])

    def deal(t, k):
        return pltpu.make_async_remote_copy(
            src_ref=part(t, k),
            dst_ref=own_block(t),
            send_sem=deal_send.at[t, k],
            recv_sem=deal_recv.at[t, k],
            device_id=plane_peer(k),
            device_id_type=pl.DeviceIdType.MESH,
        )

    def passed(t, d, k, step, sends, recvs):
        where = block(t, jnp.clip(own - step * d, 0, planes - 1), k)
        return pltpu.make_async_remote_copy(
            src_ref=where,
            dst_ref=where,
            send_sem=sends.at[t, d, k],
            recv_sem=recvs.at[t, d, k],
            device_id={"outer": jnp.clip(own + step, 0, planes - 1)},
            device_id_type=pl.DeviceIdType.MESH,
        )

    def up(t, d, k):
        return passed(t, d, k, 1, up_send, up_recv)

    def down(t, d, k):
        return passed(t, d, k, -1, down_send, down_recv)

    def share(k):
        at = pl.multiple_of((mid * 2 + low) * rows, 16)
        where = panel.at[col, pl.ds(at, rows), :]
        if k == 0:
            return pltpu.make_async_copy(tokens, where, act_own.at[0])
        return pltpu.make_async_remote_copy(
            src_ref=tokens,
            dst_ref=where,
            send_sem=act_send.at[k],
            recv_sem=act_recv.at[k],
            device_id=dict(plane_peer(k % 4), cols=sides[k // 4]),
            device_id_type=pl.DeviceIdType.MESH,
        )

    for t in range(count):
        local(t).start()
    for k in (2, 3, 1):
        for t in range(count):
            deal(t, k).start()
    for d in range(planes):
        for k in (0, 1, 2, 3):
            for t in range(count):
                if d == 0:
                    if k == 0:
                        local(t).wait()
                    else:
                        deal(t, k).wait_recv()
                if d > 0 and k < relayed[t]:

                    @pl.when(own - d >= 0)
                    def _():
                        up(t, d - 1, k).wait_recv()

                    @pl.when(own + d < planes)
                    def _():
                        down(t, d - 1, k).wait_recv()

                if d < planes - 1 and k < relayed[t]:

                    @pl.when((own - d >= 0) & has_up)
                    def _():
                        up(t, d, k).start()

                    @pl.when((own + d < planes) & has_down)
                    def _():
                        down(t, d, k).start()

        if d == 0:
            for k in (4, 5, 6, 7, 2, 3, 1, 0):
                share(k).start()
    for d in range(planes - 1):
        for k in range(4):
            for t in range(count):
                if k >= relayed[t]:
                    continue

                @pl.when((own - d >= 0) & has_up)
                def _():
                    up(t, d, k).wait_send()

                @pl.when((own + d < planes) & has_down)
                def _():
                    down(t, d, k).wait_send()

    for k in (1, 2, 3):
        for t in range(count):
            deal(t, k).wait_send()
    share(0).wait()
    for k in range(1, 8):
        share(k).wait()


def gather_all(weights, tokens, relayed):
    planes = lax.axis_size("outer")
    count = len(weights)
    depth = weights[0].shape[0]
    anywhere = pl.BlockSpec(memory_space=pl.ANY)
    line = pltpu.SemaphoreType.DMA((count, planes - 1, 4))
    shapes = [
        jax.ShapeDtypeStruct((planes * 4 * depth, weight.shape[1] // 4), weight.dtype)
        for weight in weights
    ]
    shapes.append(jax.ShapeDtypeStruct((2, 4 * tokens.shape[0], tokens.shape[1]), tokens.dtype))
    return pl.pallas_call(
        functools.partial(gather_kernel, planes, count, relayed),
        out_shape=shapes,
        in_specs=[anywhere] * (count + 1),
        out_specs=[anywhere] * (count + 1),
        scratch_shapes=[
            pltpu.SemaphoreType.DMA((count,)),
            pltpu.SemaphoreType.DMA((count, 4)),
            pltpu.SemaphoreType.DMA((count, 4)),
            line,
            line,
            line,
            line,
            pltpu.SemaphoreType.DMA((1,)),
            pltpu.SemaphoreType.DMA((8,)),
            pltpu.SemaphoreType.DMA((8,)),
        ],
        compiler_params=pltpu.CompilerParams(collective_id=0, has_side_effects=True),
        cost_estimate=pl.CostEstimate(
            flops=200_000_000_000, bytes_accessed=600_000_000, transcendentals=0
        ),
        name="gather_weights",
    )(*weights, tokens)


def plane_body(
    activations,
    positions,
    query_weight,
    key_weight,
    value_weight,
    output_weight,
    input_gain,
    query_gain,
    key_gain,
):
    rows_here, width_here = activations.shape
    inner = 4
    plane_tokens = inner * rows_here
    key_full, value_full, query_full, output_full, panel = gather_all(
        [key_weight, value_weight, query_weight, output_weight.T], activations, (4, 4, 4, 0)
    )
    own_rows = output_full.shape[0] // lax.axis_size("outer")
    mine = lax.dynamic_slice_in_dim(output_full, lax.axis_index("outer") * own_rows, own_rows, 0)
    line = along_line(mine)
    left, right = panel[0].astype(jnp.float32), panel[1].astype(jnp.float32)
    squares = jnp.sum(left * left, axis=-1) + jnp.sum(right * right, axis=-1)
    inverse = lax.rsqrt(squares[:, None] / (2 * width_here) + 1e-06)
    normed_left = (left * inverse * input_gain[:width_here]).astype(jnp.bfloat16)
    normed_right = (right * inverse * input_gain[width_here:]).astype(jnp.bfloat16)
    outer_index = lax.axis_index("outer")
    first = outer_index * plane_tokens
    own_positions = lax.dynamic_slice_in_dim(positions, first, plane_tokens, 0)

    def project(weight):
        return jnp.dot(
            normed_left, weight[:width_here], preferred_element_type=jnp.float32
        ) + jnp.dot(normed_right, weight[width_here:], preferred_element_type=jnp.float32)

    key_raw = project(key_full)
    keys = rotate(head_norm(key_raw.reshape(plane_tokens, -1, HD), key_gain), own_positions)
    keys = keys.astype(jnp.bfloat16).reshape(plane_tokens, -1)
    keys_before = passed_along(keys[plane_tokens - WINDOW :], "outer", 1)
    values = project(value_full).astype(jnp.bfloat16)
    values_before = passed_along(values[plane_tokens - WINDOW :], "outer", 1)
    all_keys = jnp.concatenate([keys_before, keys], axis=0)
    all_values = jnp.concatenate([values_before, values], axis=0)
    queries = rotate(
        head_norm(project(query_full).reshape(plane_tokens, -1, HD), query_gain), own_positions
    )
    queries = queries.astype(jnp.bfloat16).reshape(plane_tokens, -1)
    padded = jnp.concatenate([jnp.zeros((WINDOW,), jnp.int32), positions], axis=0)
    key_positions = lax.dynamic_slice_in_dim(padded, first, plane_tokens + WINDOW, 0)
    count = rows_here + WINDOW
    contexts = []
    for block in range(inner):
        at = block * rows_here
        contexts.append(
            attend(
                queries[at : at + rows_here],
                all_keys[at : at + count],
                all_values[at : at + count],
                first + at + jnp.arange(rows_here, dtype=jnp.int32),
                first + at - WINDOW + jnp.arange(count, dtype=jnp.int32),
                own_positions[at : at + rows_here],
                key_positions[at : at + count],
            )
        )
    for d in range(1, lax.axis_size("outer")):
        output_full = lax.dynamic_update_slice_in_dim(
            output_full, line[d - 1], plane_of(d) * own_rows, 0
        )
    half = rows_here // 2

    def projected(at):
        context = jnp.concatenate([block[at : at + half] for block in contexts], axis=0)
        terms = lax.dot_general(
            context, output_full, (((1,), (1,)), ((), ())), preferred_element_type=jnp.float32
        )
        return terms.astype(jnp.bfloat16).reshape(2, 2, half, -1)

    summed = reduce_in_plane(projected(0), projected(half), width_here)
    return (activations.astype(jnp.float32) + summed).astype(jnp.bfloat16)


def plane_solution(mesh):
    sizes = mesh.shape
    split = Mesh(
        mesh.devices.reshape(
            sizes["groups"], sizes["rows"] // 4, 2, 2, sizes["cols"], sizes["sub"]
        ),
        ("groups", "outer", "mid", "low", "cols", "sub"),
    )
    rows, cols = ("outer", "mid", "low"), ("cols", "sub")
    placed = (
        P(("groups",) + rows, cols),
        P("groups"),
        P(rows, cols),
        P(rows, cols),
        P(rows, cols),
        P(cols, rows),
        P(),
        P(),
        P(),
    )
    return jax.shard_map(
        plane_body,
        mesh=split,
        in_specs=placed,
        out_specs=P(("groups",) + rows, cols),
        check_vma=False,
    )


def solution(mesh):
    sizes = mesh.shape
    parts = sizes["cols"] * sizes["sub"]

    def run(*args):
        tokens = args[0].shape[0] // (sizes["groups"] * sizes["rows"])
        kv_heads = args[3].shape[1] // (HD * parts)
        fits = sizes["rows"] % (4 * parts) == 0 and kv_heads % 4 == 0
        fits = fits and sizes["cols"] == 2 and sizes["sub"] == 1 and tokens * 4 >= WINDOW
        plan = plane_solution(mesh) if fits else row_solution(mesh)
        return plan(*args)

    return run
```
